32 devices in a mesh: tile: 8 (over z, y), rcpt: 4 (over x, core).
Axes of the slice: x: 2, y: 2, z: 4, core: 2. Of those that a mesh axis runs over, the one named last changes fastest.
Arguments:
- adjoint_state: float32 [64, 16, 128, 256], P('rcpt', None, 'tile'), may hold values from -6 to 6
- met_fields: bfloat16 [12, 3, 16, 128, 256], P(None, None, 'rcpt', 'tile'), may hold values from -0.34960938 to 0.34960938
- forcing: bfloat16 [64, 128, 256], P(None, 'tile'), may hold values from -6 to 6
- cluster_ids: int32 [64], P('rcpt'), may hold values from 0 to 63
- hour_index: int32 [2], replicated, may hold values from 0 to 11
Outputs:
- adjoint_out: float32 [64, 16, 128, 256], P('rcpt', None, 'tile')
The draws below stay inside these ranges and needn't reach their ends.
All inputs are finite; a program needn't handle non-finite values.
Results may differ from the reference program's by a relative error of at most 0.00035.
Values may be sent and summed in bfloat16 or wider, within the bound.
A program may use at most 64 MiB of HBM per device.

```python
import jax
import jax.numpy as jnp
from jax import lax

TRACERS = 64
CLUSTERS = 64
LEV = 16
LAT = 256
HOURS = 12
STEPS = 2
NLON = 128


def place_ends(array, stream_key, smallest, largest):
    longest = array.shape.index(max(array.shape))
    spots = []
    for shift in (0, 1):
        where = [jax.random.randint(jax.random.fold_in(stream_key, axis), (), 0, length) for axis, length in enumerate(array.shape)]
        where[longest] = (where[longest] + shift) % array.shape[longest]
        spots.append(tuple(where))
    return array.at[spots[0]].set(smallest).at[spots[1]].set(largest)


def block_levels(rng, dims, pieces, low, largest):
    def one(dim, parts):
        draws = jax.random.uniform(jax.random.fold_in(jax.random.fold_in(rng, 6), dim), (parts,), jnp.float32, low / len(pieces), largest / len(pieces))
        return jnp.repeat(jnp.exp(draws), dims[dim] // parts).reshape((-1,) + (1,) * (len(dims) - dim - 1))

    level = one(*pieces[0])
    for cut in pieces[1:]:
        level = level * one(*cut)
    return level


def centred(key, shape, scale, bound, cuts=(), dtype=jnp.bfloat16):
    level = block_levels(key, shape, cuts, -0.22, 0.18) if cuts else 1.0
    drawn = jax.random.normal(key, shape, jnp.float32) * scale * level
    return jnp.minimum(jnp.maximum(drawn, -bound), bound).astype(dtype)


def setup_inputs(seed: int = 0) -> dict:
    arg_keys = jax.random.split(jax.random.key(seed), 6)
    adjoint_state = centred(arg_keys[0], (TRACERS, LEV, NLON, LAT), 1.0, 6.0, ((0, 4), (2, 8)), jnp.float32)
    met_fields = jnp.clip(jax.random.uniform(arg_keys[1], (HOURS, 3, LEV, NLON, LAT), jnp.float32, -0.34960938, 0.34960938) * block_levels(arg_keys[1], (HOURS, 3, LEV, NLON, LAT), ((2, 4), (3, 8)), -0.4, 0.0), -0.34960938, 0.34960938).astype(jnp.bfloat16)
    forcing = centred(arg_keys[2], (CLUSTERS, NLON, LAT), 1.0, 6.0, ((1, 8),))
    cluster_ids = place_ends(jax.random.randint(arg_keys[3], (TRACERS,), 0, CLUSTERS), jax.random.fold_in(arg_keys[3], 1), 0, CLUSTERS - 1).astype(jnp.int32)
    hour_index = jax.random.randint(arg_keys[4], (STEPS,), 0, HOURS).astype(jnp.int32)
    return dict(adjoint_state=adjoint_state, met_fields=met_fields, forcing=forcing, cluster_ids=cluster_ids, hour_index=hour_index)


def horizontal(lam, winds):
    cx = winds[0].astype(jnp.float32)
    cy = winds[1].astype(jnp.float32)
    px = lam * jnp.maximum(cx, 0.0)
    mx = lam * jnp.minimum(cx, 0.0)
    py = lam * jnp.maximum(cy, 0.0)
    my = lam * jnp.minimum(cy, 0.0)
    east = jnp.roll(px, -1, axis=2)
    west = jnp.roll(mx, 1, axis=2)
    zero = jnp.zeros_like(py[..., :1])
    north = jnp.concatenate([py[..., 1:], zero], axis=3)
    south = jnp.concatenate([zero, my[..., :-1]], axis=3)
    return lam * (1.0 - jnp.abs(cx) - jnp.abs(cy)) + east - west + north - south


def vertical(lam, mixing):
    coeff = 0.02 + 0.25 * jnp.abs(mixing.astype(jnp.float32))
    flux = coeff[:-1] * (lam[:, 1:] - lam[:, :-1])
    zero = jnp.zeros_like(flux[:, :1])
    return jnp.concatenate([flux, zero], axis=1) - jnp.concatenate([zero, flux], axis=1)


def reference(adjoint_state, met_fields, forcing, cluster_ids, hour_index):
    rows = forcing[cluster_ids].astype(jnp.float32)
    lam = adjoint_state
    for step in range(STEPS):
        metnow = lax.dynamic_index_in_dim(met_fields, hour_index[step], 0, keepdims=False)
        state = horizontal(lam, metnow) + vertical(lam, metnow[2])
        lam = state.at[:, -1].add(rows)
    return lam
```

```python
import functools

import jax
import jax.numpy as jnp
from jax import lax
from jax.experimental import pallas as pl
from jax.experimental.pallas import tpu as pltpu
from jax.sharding import PartitionSpec as P

STEPS = 2
F32 = jnp.float32
BF16 = jnp.bfloat16
MESH = pl.DeviceIdType.MESH


def mixing_of(m):
    return 0.02 + 0.25 * jnp.abs(m.astype(F32))


def shifted(x, by, axis):
    return pltpu.roll(x, (-by) % x.shape[axis], axis)


def latitude_coeffs(cy):
    lane = lax.broadcasted_iota(jnp.int32, cy.shape, 1)
    north = jnp.where(lane == cy.shape[1] - 1, 0.0, shifted(jnp.maximum(cy, 0.0), 1, 1))
    south = jnp.where(lane == 0, 0.0, shifted(-jnp.minimum(cy, 0.0), -1, 1))
    return north, south


def level_coeffs(met, k, levels):
    cx = met(0, k).astype(F32)
    cy = met(1, k).astype(F32)
    below = jnp.maximum(k - 1, 0)
    up = mixing_of(met(2, k)) * (k < levels - 1).astype(F32)
    down = mixing_of(met(2, below)) * (k > 0).astype(F32)
    row = lax.broadcasted_iota(jnp.int32, cx.shape, 0)
    east = jnp.where(row == cx.shape[0] - 1, 0.0, shifted(jnp.maximum(cx, 0.0), 1, 0))
    west = jnp.where(row == 0, 0.0, shifted(-jnp.minimum(cx, 0.0), -1, 0))
    north, south = latitude_coeffs(cy)
    centre = 1.0 - jnp.abs(cx) - jnp.abs(cy) - up - down
    return centre, up, down, east, west, north, south


def advance(lam, above, below, coeffs):
    centre, up, down, east, west, north, south = coeffs
    out = lam * centre + (above * up + below * down)
    out += shifted(lam, 1, 0) * east + shifted(lam, -1, 0) * west
    out += shifted(lam, 1, 1) * north + shifted(lam, -1, 1) * south
    return out


def first_step(
    tiles,
    ranks,
    hour_ref,
    ids_ref,
    lam_hbm,
    met_ref,
    forcing_ref,
    lam1_hbm,
    met1_ref,
    halo_ref,
    rows_ref,
    lam,
    lam1,
    met0,
    edges,
    lam_out,
    lam_in,
    cx_out,
    cx_in,
    flux_out,
    columns,
    lam_sem,
    out_sem,
    gsend,
    grecv,
    hsend,
    hrecv,
):
    tracers, levels, lons, _ = lam.shape
    share = levels // ranks
    tile, rank = lax.axis_index("tile"), lax.axis_index("rcpt")
    east, west = lax.rem(tile + 1, tiles), lax.rem(tile + tiles - 1, tiles)
    last = lons - 1

    load = pltpu.make_async_copy(lam_hbm, lam, lam_sem)
    load.start()

    bits = []
    b = ranks // 2
    while b:
        bits.append(b)
        b //= 2
    barrier = pltpu.get_barrier_semaphore()
    for other in (east, west):
        pl.semaphore_signal(barrier, inc=1, device_id=(other, rank), device_id_type=MESH)
    for b in bits:
        pl.semaphore_signal(barrier, inc=1, device_id=(tile, rank ^ b), device_id_type=MESH)

    mine = pl.ds(rank * share, share)
    met0[:, mine] = met_ref[hour_ref[0]]
    met1_ref[:, mine] = met_ref[hour_ref[1]]

    pl.semaphore_wait(barrier, 2 + len(bits))

    gathers = {}

    def send_block(step, offset, b):
        buf = (met0, met1_ref)[step]
        where = pl.ds((rank ^ offset) * share, share)
        copy = pltpu.make_async_remote_copy(
            src_ref=buf.at[:, where],
            dst_ref=buf.at[:, where],
            send_sem=gsend.at[step, offset ^ b],
            recv_sem=grecv.at[step, offset ^ b],
            device_id=(tile, rank ^ b),
            device_id_type=MESH,
        )
        copy.start()
        gathers[step, offset ^ b] = copy

    def arrived(step, offset):
        buf = (met0, met1_ref)[step]
        where = pl.ds((rank ^ offset) * share, share)
        pltpu.make_async_remote_copy(
            src_ref=buf.at[:, where],
            dst_ref=buf.at[:, where],
            send_sem=gsend.at[step, offset],
            recv_sem=grecv.at[step, offset],
            device_id=(tile, rank ^ offset),
            device_id_type=MESH,
        ).wait_recv()

    def spread(step, offset, after):
        for i in range(after, len(bits)):
            send_block(step, offset, bits[i])

    def forward(step):
        for offset in order:
            arrived(step, offset)
            low = offset & -offset
            spread(step, offset, bits.index(low) + 1)

    order = sorted(range(1, ranks), key=lambda o: (bin(o).count("1"), -o))

    spread(0, 0, 0)

    load.wait()

    def pick(t, _):
        for n, c in enumerate((0, 1, last - 1, last)):
            edges[n, t] = lam[t, :, c, :]
        lam_out[0, t] = edges[0, t].astype(BF16)
        lam_out[1, t] = edges[3, t].astype(BF16)
        return 0

    lax.fori_loop(0, tracers, pick, 0)

    def halo_copy(n, src, dst, side):
        return pltpu.make_async_remote_copy(
            src_ref=src.at[side],
            dst_ref=dst.at[side],
            send_sem=hsend.at[n, side],
            recv_sem=hrecv.at[n, side],
            device_id=((west, east)[side], rank),
            device_id_type=MESH,
        )

    lam_copies = [halo_copy(0, lam_out, lam_in, side) for side in (0, 1)]
    for c in lam_copies:
        c.start()

    def source(t, _):
        rows_ref[t] = forcing_ref[ids_ref[t]]
        return 0

    lax.fori_loop(0, tracers, source, 0)

    forward(0)
    spread(1, 0, 0)

    def pick_met(k, _):
        cx = met0[0, k].astype(F32)
        cy = met0[1, k].astype(F32)
        kz = met0[2, k].astype(F32)
        rows = [cx[0:1], cx[1:2], cx[last - 1 : last], cx[last : last + 1]]
        rows += [cy[0:1], cy[last : last + 1], kz[0:1], kz[last : last + 1]]
        for n, r in enumerate(rows):
            columns[n, pl.ds(k, 1), :] = r
        return 0

    lax.fori_loop(0, levels, pick_met, 0)
    cx_out[0] = columns[0].astype(BF16)
    cx_out[1] = columns[3].astype(BF16)
    cx_copies = [halo_copy(1, cx_out, cx_in, side) for side in (0, 1)]
    for c in cx_copies:
        c.start()

    group = 4 if tracers % 4 == 0 else 1

    def level(k, _):
        coeffs = level_coeffs(lambda f, n: met0[f, n], k, levels)
        above = jnp.minimum(k + 1, levels - 1)
        below = jnp.maximum(k - 1, 0)

        def some(g, _):
            for u in range(group):
                t = g * group + u
                lam1[t, k] = advance(lam[t, k], lam[t, above], lam[t, below], coeffs)
            return 0

        lax.fori_loop(0, tracers // group, some, 0)
        return 0

    lax.fori_loop(0, levels, level, 0)

    def add_rows(t, _):
        lam1[t, levels - 1] += rows_ref[t].astype(F32)
        return 0

    lax.fori_loop(0, tracers, add_rows, 0)

    forward(1)

    def pick_next(k, _):
        cx = met1_ref[0, k].astype(F32)
        columns[8, pl.ds(k, 1), :] = cx[0:1]
        columns[9, pl.ds(k, 1), :] = cx[last : last + 1]
        return 0

    lax.fori_loop(0, levels, pick_next, 0)

    for c in cx_copies + lam_copies:
        c.wait()

    def edge_coeffs(side):
        cx = columns[(0, 3)[side]]
        cy = columns[4 + side]
        kz = mixing_of(columns[6 + side])
        row = lax.broadcasted_iota(jnp.int32, kz.shape, 0)
        up = jnp.where(row == levels - 1, 0.0, kz)
        down = shifted(up, -1, 0)
        north, south = latitude_coeffs(cy)
        if side == 0:
            from_east = jnp.maximum(columns[1], 0.0)
            from_west = -jnp.minimum(cx_in[1].astype(F32), 0.0)
            leaves = jnp.maximum(columns[8], 0.0)
        else:
            from_east = jnp.maximum(cx_in[0].astype(F32), 0.0)
            from_west = -jnp.minimum(columns[2], 0.0)
            leaves = -jnp.minimum(columns[9], 0.0)
        centre = 1.0 - jnp.abs(cx) - jnp.abs(cy) - up - down
        return centre, up, down, from_east, from_west, north, south, leaves

    flux_copies = []
    for side in (0, 1):
        centre, up, down, from_east, from_west, north, south, leaves = edge_coeffs(side)
        top = lax.broadcasted_iota(jnp.int32, centre.shape, 0) == levels - 1
        c = (0, last)[side]

        def edge(t, _):
            x = edges[(0, 3)[side], t]
            if side == 0:
                e, w = edges[1, t], lam_in[1, t].astype(F32)
            else:
                e, w = lam_in[0, t].astype(F32), edges[2, t]
            out = x * centre + shifted(x, 1, 0) * up + shifted(x, -1, 0) * down
            out += e * from_east + w * from_west
            out += shifted(x, 1, 1) * north + shifted(x, -1, 1) * south
            out += jnp.where(top, rows_ref[t].astype(F32)[c : c + 1], 0.0)
            flux_out[side, t] = (out * leaves).astype(BF16)
            lam1[t, :, c, :] = out
            return 0

        lax.fori_loop(0, tracers, edge, 0)
        copy = halo_copy(2, flux_out, halo_ref, side)
        copy.start()
        flux_copies.append(copy)

    store = pltpu.make_async_copy(lam1, lam1_hbm, out_sem)
    store.start()
    for copy in gathers.values():
        copy.wait_send()
    for copy in flux_copies:
        copy.wait()
    store.wait()


def second_step(lam_ref, met_ref, halo_ref, rows_ref, out_ref, halo):
    tracers, levels, lons, _ = lam_ref.shape
    halo[...] = halo_ref[...].astype(F32)
    row = lax.broadcasted_iota(jnp.int32, lam_ref.shape[2:], 0)

    def level(k, _):
        coeffs = level_coeffs(lambda f, n: met_ref[f, n], k, levels)
        above = jnp.minimum(k + 1, levels - 1)
        below = jnp.maximum(k - 1, 0)
        for t in range(tracers):
            out = advance(lam_ref[t, k], lam_ref[t, above], lam_ref[t, below], coeffs)
            out += jnp.where(row == lons - 1, halo[0, t, pl.ds(k, 1), :], 0.0)
            out += jnp.where(row == 0, halo[1, t, pl.ds(k, 1), :], 0.0)
            out_ref[t, k] = out
        return 0

    lax.fori_loop(0, levels, level, 0)
    for t in range(tracers):
        out_ref[t, levels - 1] += rows_ref[t].astype(F32)


def per_device(tiles, ranks, adjoint_state, met_fields, forcing, cluster_ids, hour_index):
    tracers, levels, lons, lats = adjoint_state.shape
    fields = met_fields.shape[1]
    vmem = pl.BlockSpec(memory_space=pltpu.VMEM)
    smem = pl.BlockSpec(memory_space=pltpu.SMEM)
    hbm = pl.BlockSpec(memory_space=pl.ANY)
    both = (2, tracers, levels, lats)
    lam1, met1, halo, rows = pl.pallas_call(
        functools.partial(first_step, tiles, ranks),
        out_shape=(
            jax.ShapeDtypeStruct(adjoint_state.shape, F32),
            jax.ShapeDtypeStruct((fields, levels, lons, lats), BF16),
            jax.ShapeDtypeStruct(both, BF16),
            jax.ShapeDtypeStruct((tracers, lons, lats), BF16),
        ),
        in_specs=[smem, smem, hbm, vmem, vmem],
        out_specs=(hbm, vmem, vmem, vmem),
        scratch_shapes=[
            pltpu.VMEM(adjoint_state.shape, F32),
            pltpu.VMEM(adjoint_state.shape, F32),
            pltpu.VMEM((fields, levels, lons, lats), BF16),
            pltpu.VMEM((4, tracers, levels, lats), F32),
            pltpu.VMEM(both, BF16),
            pltpu.VMEM(both, BF16),
            pltpu.VMEM((2, levels, lats), BF16),
            pltpu.VMEM((2, levels, lats), BF16),
            pltpu.VMEM(both, BF16),
            pltpu.VMEM((10, levels, lats), F32),
            pltpu.SemaphoreType.DMA,
            pltpu.SemaphoreType.DMA,
            pltpu.SemaphoreType.DMA((STEPS, ranks)),
            pltpu.SemaphoreType.DMA((STEPS, ranks)),
            pltpu.SemaphoreType.DMA((3, 2)),
            pltpu.SemaphoreType.DMA((3, 2)),
        ],
        compiler_params=pltpu.CompilerParams(
            collective_id=0, has_side_effects=True, vmem_limit_bytes=40 << 20
        ),
        name="first_step",
    )(hour_index, cluster_ids, adjoint_state, met_fields, forcing)

    block = 4 if tracers % 4 == 0 else 1
    state = pl.BlockSpec((block, levels, lons, lats), lambda t: (t, 0, 0, 0))
    return pl.pallas_call(
        second_step,
        grid=(tracers // block,),
        out_shape=jax.ShapeDtypeStruct(adjoint_state.shape, F32),
        in_specs=[
            state,
            pl.BlockSpec(met1.shape, lambda t: (0, 0, 0, 0)),
            pl.BlockSpec((2, block, levels, lats), lambda t: (0, t, 0, 0)),
            pl.BlockSpec((block, lons, lats), lambda t: (t, 0, 0)),
        ],
        out_specs=state,
        scratch_shapes=[pltpu.VMEM((2, block, levels, lats), F32)],
        compiler_params=pltpu.CompilerParams(vmem_limit_bytes=40 << 20),
        name="second_step",
    )(lam1, met1, halo, rows)


def solution(mesh):
    placed = (
        P("rcpt", None, "tile", None),
        P(None, None, "rcpt", "tile", None),
        P(None, "tile", None),
        P("rcpt"),
        P(),
    )
    return jax.shard_map(
        functools.partial(per_device, mesh.shape["tile"], mesh.shape["rcpt"]),
        mesh=mesh,
        in_specs=placed,
        out_specs=P("rcpt", None, "tile", None),
        check_vma=False,
    )
```

```python
import functools

import jax
import jax.numpy as jnp
from jax import lax
from jax.experimental import pallas as pl
from jax.experimental.pallas import tpu as pltpu
from jax.sharding import PartitionSpec as P

STEPS = 2
F32 = jnp.float32
BF16 = jnp.bfloat16
MESH = pl.DeviceIdType.MESH


def mixing_of(m):
    return 0.02 + 0.25 * jnp.abs(m.astype(F32))


def shifted(x, by, axis):
    return pltpu.roll(x, (-by) % x.shape[axis], axis)


def latitude_coeffs(cy):
    lane = lax.broadcasted_iota(jnp.int32, cy.shape, 1)
    north = jnp.where(lane == cy.shape[1] - 1, 0.0, shifted(jnp.maximum(cy, 0.0), 1, 1))
    south = jnp.where(lane == 0, 0.0, shifted(-jnp.minimum(cy, 0.0), -1, 1))
    return north, south


def level_coeffs(met, k, levels):
    cx = met(0, k).astype(F32)
    cy = met(1, k).astype(F32)
    below = jnp.maximum(k - 1, 0)
    up = mixing_of(met(2, k)) * (k < levels - 1).astype(F32)
    down = mixing_of(met(2, below)) * (k > 0).astype(F32)
    row = lax.broadcasted_iota(jnp.int32, cx.shape, 0)
    east = jnp.where(row == cx.shape[0] - 1, 0.0, shifted(jnp.maximum(cx, 0.0), 1, 0))
    west = jnp.where(row == 0, 0.0, shifted(-jnp.minimum(cx, 0.0), -1, 0))
    north, south = latitude_coeffs(cy)
    centre = 1.0 - jnp.abs(cx) - jnp.abs(cy) - up - down
    return centre, up, down, east, west, north, south


def advance(lam, above, below, coeffs):
    centre, up, down, east, west, north, south = coeffs
    out = lam * centre + (above * up + below * down)
    out += shifted(lam, 1, 0) * east + shifted(lam, -1, 0) * west
    out += shifted(lam, 1, 1) * north + shifted(lam, -1, 1) * south
    return out


def first_step(
    tiles,
    ranks,
    hour_hbm,
    ids_hbm,
    lam_hbm,
    met_hbm,
    forcing_hbm,
    lam1,
    met1_ref,
    halo_ref,
    rows_ref,
    hour_ref,
    ids_ref,
    lam,
    met_ref,
    forcing_ref,
    met0,
    edges,
    lam_out,
    lam_in,
    cx_out,
    cx_in,
    flux_out,
    columns,
    load_sem,
    gsend,
    grecv,
    hsend,
    hrecv,
):
    tracers, levels, lons, _ = lam.shape
    share = levels // ranks
    tile, rank = lax.axis_index("tile"), lax.axis_index("rcpt")
    east, west = lax.rem(tile + 1, tiles), lax.rem(tile + tiles - 1, tiles)
    last = lons - 1

    pairs = ((hour_hbm, hour_ref), (met_hbm, met_ref), (lam_hbm, lam))
    pairs += ((ids_hbm, ids_ref), (forcing_hbm, forcing_ref))
    loads = [pltpu.make_async_copy(*pair, load_sem.at[n]) for n, pair in enumerate(pairs)]
    for load in loads:
        load.start()

    bits = []
    b = ranks // 2
    while b:
        bits.append(b)
        b //= 2
    barrier = pltpu.get_barrier_semaphore()
    for other in (east, west):
        pl.semaphore_signal(barrier, inc=1, device_id=(other, rank), device_id_type=MESH)
    for b in bits:
        pl.semaphore_signal(barrier, inc=1, device_id=(tile, rank ^ b), device_id_type=MESH)

    loads[0].wait()
    loads[1].wait()
    mine = pl.ds(rank * share, share)
    met0[:, mine] = met_ref[hour_ref[0]]
    met1_ref[:, mine] = met_ref[hour_ref[1]]

    pl.semaphore_wait(barrier, 2 + len(bits))

    gathers = {}

    def send_block(step, offset, b):
        buf = (met0, met1_ref)[step]
        where = pl.ds((rank ^ offset) * share, share)
        copy = pltpu.make_async_remote_copy(
            src_ref=buf.at[:, where],
            dst_ref=buf.at[:, where],
            send_sem=gsend.at[step, offset ^ b],
            recv_sem=grecv.at[step, offset ^ b],
            device_id=(tile, rank ^ b),
            device_id_type=MESH,
        )
        copy.start()
        gathers[step, offset ^ b] = copy

    def arrived(step, offset):
        buf = (met0, met1_ref)[step]
        where = pl.ds((rank ^ offset) * share, share)
        pltpu.make_async_remote_copy(
            src_ref=buf.at[:, where],
            dst_ref=buf.at[:, where],
            send_sem=gsend.at[step, offset],
            recv_sem=grecv.at[step, offset],
            device_id=(tile, rank ^ offset),
            device_id_type=MESH,
        ).wait_recv()

    def spread(step, offset, after):
        for i in range(after, len(bits)):
            send_block(step, offset, bits[i])

    def forward(step, which):
        for offset in which:
            arrived(step, offset)
            low = offset & -offset
            spread(step, offset, bits.index(low) + 1)

    order = sorted(range(1, ranks), key=lambda o: (bin(o).count("1"), -o))
    passed_on = [o for o in order if o % 2 == 0]
    kept = [o for o in order if o % 2]

    spread(0, 0, 0)

    loads[2].wait()

    def pick(t, _):
        for n, c in enumerate((0, 1, last - 1, last)):
            edges[n, t] = lam[t, :, c, :]
        lam_out[0, t] = edges[0, t].astype(BF16)
        lam_out[1, t] = edges[3, t].astype(BF16)
        return 0

    lax.fori_loop(0, tracers, pick, 0)

    def halo_copy(n, src, dst, side):
        return pltpu.make_async_remote_copy(
            src_ref=src.at[side],
            dst_ref=dst.at[side],
            send_sem=hsend.at[n, side],
            recv_sem=hrecv.at[n, side],
            device_id=((west, east)[side], rank),
            device_id_type=MESH,
        )

    lam_copies = [halo_copy(0, lam_out, lam_in, side) for side in (0, 1)]
    for c in lam_copies:
        c.start()

    loads[3].wait()
    loads[4].wait()

    def source(t, _):
        rows_ref[t] = forcing_ref[ids_ref[t]]
        return 0

    lax.fori_loop(0, tracers, source, 0)

    forward(0, order)
    spread(1, 0, 0)

    def pick_met(k, _):
        cx = met0[0, k].astype(F32)
        cy = met0[1, k].astype(F32)
        kz = met0[2, k].astype(F32)
        rows = [cx[0:1], cx[1:2], cx[last - 1 : last], cx[last : last + 1]]
        rows += [cy[0:1], cy[last : last + 1], kz[0:1], kz[last : last + 1]]
        for n, r in enumerate(rows):
            columns[n, pl.ds(k, 1), :] = r
        return 0

    lax.fori_loop(0, levels, pick_met, 0)
    cx_out[0] = columns[0].astype(BF16)
    cx_out[1] = columns[3].astype(BF16)
    cx_copies = [halo_copy(1, cx_out, cx_in, side) for side in (0, 1)]
    for c in cx_copies:
        c.start()

    group = 4 if tracers % 4 == 0 else 1

    def level(k, _):
        coeffs = level_coeffs(lambda f, n: met0[f, n], k, levels)
        above = jnp.minimum(k + 1, levels - 1)
        below = jnp.maximum(k - 1, 0)

        def some(g, _):
            for u in range(group):
                t = g * group + u
                lam1[t, k] = advance(lam[t, k], lam[t, above], lam[t, below], coeffs)
            return 0

        lax.fori_loop(0, tracers // group, some, 0)
        return 0

    lax.fori_loop(0, levels // 2, level, 0)
    forward(1, passed_on)
    lax.fori_loop(levels // 2, levels, level, 0)

    def add_rows(t, _):
        lam1[t, levels - 1] += rows_ref[t].astype(F32)
        return 0

    lax.fori_loop(0, tracers, add_rows, 0)

    forward(1, kept)

    def pick_next(k, _):
        cx = met1_ref[0, k].astype(F32)
        columns[8, pl.ds(k, 1), :] = cx[0:1]
        columns[9, pl.ds(k, 1), :] = cx[last : last + 1]
        return 0

    lax.fori_loop(0, levels, pick_next, 0)

    for c in cx_copies + lam_copies:
        c.wait()

    def edge_coeffs(side):
        cx = columns[(0, 3)[side]]
        cy = columns[4 + side]
        kz = mixing_of(columns[6 + side])
        row = lax.broadcasted_iota(jnp.int32, kz.shape, 0)
        up = jnp.where(row == levels - 1, 0.0, kz)
        down = shifted(up, -1, 0)
        north, south = latitude_coeffs(cy)
        if side == 0:
            from_east = jnp.maximum(columns[1], 0.0)
            from_west = -jnp.minimum(cx_in[1].astype(F32), 0.0)
            leaves = jnp.maximum(columns[8], 0.0)
        else:
            from_east = jnp.maximum(cx_in[0].astype(F32), 0.0)
            from_west = -jnp.minimum(columns[2], 0.0)
            leaves = -jnp.minimum(columns[9], 0.0)
        centre = 1.0 - jnp.abs(cx) - jnp.abs(cy) - up - down
        return centre, up, down, from_east, from_west, north, south, leaves

    flux_copies = []
    for side in (0, 1):
        centre, up, down, from_east, from_west, north, south, leaves = edge_coeffs(side)
        top = lax.broadcasted_iota(jnp.int32, centre.shape, 0) == levels - 1
        c = (0, last)[side]

        def edge(t, _):
            x = edges[(0, 3)[side], t]
            if side == 0:
                e, w = edges[1, t], lam_in[1, t].astype(F32)
            else:
                e, w = lam_in[0, t].astype(F32), edges[2, t]
            out = x * centre + shifted(x, 1, 0) * up + shifted(x, -1, 0) * down
            out += e * from_east + w * from_west
            out += shifted(x, 1, 1) * north + shifted(x, -1, 1) * south
            out += jnp.where(top, rows_ref[t].astype(F32)[c : c + 1], 0.0)
            flux_out[side, t] = (out * leaves).astype(BF16)
            lam1[t, :, c, :] = out
            return 0

        lax.fori_loop(0, tracers, edge, 0)
        copy = halo_copy(2, flux_out, halo_ref, side)
        copy.start()
        flux_copies.append(copy)

    for copy in gathers.values():
        copy.wait_send()
    for copy in flux_copies:
        copy.wait()


def second_step(lam_ref, met_ref, halo_ref, rows_ref, out_ref, halo):
    _, levels, lons, _ = lam_ref.shape
    tracers = out_ref.shape[0]
    first = pl.program_id(0) * tracers
    halo[...] = halo_ref[:, pl.ds(first, tracers)].astype(F32)
    row = lax.broadcasted_iota(jnp.int32, lam_ref.shape[2:], 0)

    def level(k, _):
        coeffs = level_coeffs(lambda f, n: met_ref[f, n], k, levels)
        above = jnp.minimum(k + 1, levels - 1)
        below = jnp.maximum(k - 1, 0)
        for t in range(tracers):
            x = lam_ref[first + t, k]
            out = advance(x, lam_ref[first + t, above], lam_ref[first + t, below], coeffs)
            out += jnp.where(row == lons - 1, halo[0, t, pl.ds(k, 1), :], 0.0)
            out += jnp.where(row == 0, halo[1, t, pl.ds(k, 1), :], 0.0)
            out_ref[t, k] = out
        return 0

    lax.fori_loop(0, levels, level, 0)
    for t in range(tracers):
        out_ref[t, levels - 1] += rows_ref[first + t].astype(F32)


def per_device(tiles, ranks, adjoint_state, met_fields, forcing, cluster_ids, hour_index):
    tracers, levels, lons, lats = adjoint_state.shape
    fields = met_fields.shape[1]
    vmem = pl.BlockSpec(memory_space=pltpu.VMEM)
    hbm = pl.BlockSpec(memory_space=pltpu.HBM)
    both = (2, tracers, levels, lats)
    arrays = (hour_index, cluster_ids, adjoint_state, met_fields, forcing)
    arrays = [pltpu.with_memory_space_constraint(x, pltpu.HBM) for x in arrays]
    lam1, met1, halo, rows = pl.pallas_call(
        functools.partial(first_step, tiles, ranks),
        out_shape=(
            jax.ShapeDtypeStruct(adjoint_state.shape, F32),
            jax.ShapeDtypeStruct((fields, levels, lons, lats), BF16),
            jax.ShapeDtypeStruct(both, BF16),
            jax.ShapeDtypeStruct((tracers, lons, lats), BF16),
        ),
        in_specs=[hbm] * 5,
        out_specs=(vmem,) * 4,
        scratch_shapes=[
            pltpu.SMEM(hour_index.shape, jnp.int32),
            pltpu.SMEM(cluster_ids.shape, jnp.int32),
            pltpu.VMEM(adjoint_state.shape, F32),
            pltpu.VMEM(met_fields.shape, BF16),
            pltpu.VMEM(forcing.shape, BF16),
            pltpu.VMEM((fields, levels, lons, lats), BF16),
            pltpu.VMEM((4, tracers, levels, lats), F32),
            pltpu.VMEM(both, BF16),
            pltpu.VMEM(both, BF16),
            pltpu.VMEM((2, levels, lats), BF16),
            pltpu.VMEM((2, levels, lats), BF16),
            pltpu.VMEM(both, BF16),
            pltpu.VMEM((10, levels, lats), F32),
            pltpu.SemaphoreType.DMA((5,)),
            pltpu.SemaphoreType.DMA((STEPS, ranks)),
            pltpu.SemaphoreType.DMA((STEPS, ranks)),
            pltpu.SemaphoreType.DMA((3, 2)),
            pltpu.SemaphoreType.DMA((3, 2)),
        ],
        compiler_params=pltpu.CompilerParams(
            collective_id=0, has_side_effects=True, vmem_limit_bytes=40 << 20
        ),
        name="first_step",
    )(*arrays)

    block = 4 if tracers % 4 == 0 else 1
    state = pl.BlockSpec((block, levels, lons, lats), lambda t: (t, 0, 0, 0))
    return pl.pallas_call(
        second_step,
        grid=(tracers // block,),
        out_shape=jax.ShapeDtypeStruct(adjoint_state.shape, F32),
        in_specs=[vmem] * 4,
        out_specs=state,
        scratch_shapes=[pltpu.VMEM((2, block, levels, lats), F32)],
        compiler_params=pltpu.CompilerParams(vmem_limit_bytes=40 << 20),
        name="second_step",
    )(lam1, met1, halo, rows)


def solution(mesh):
    placed = (
        P("rcpt", None, "tile", None),
        P(None, None, "rcpt", "tile", None),
        P(None, "tile", None),
        P("rcpt"),
        P(),
    )
    return jax.shard_map(
        functools.partial(per_device, mesh.shape["tile"], mesh.shape["rcpt"]),
        mesh=mesh,
        in_specs=placed,
        out_specs=P("rcpt", None, "tile", None),
        check_vma=False,
    )
```

```python
import functools

import jax
import jax.numpy as jnp
from jax import lax
from jax.experimental import pallas as pl
from jax.experimental.pallas import tpu as pltpu
from jax.sharding import PartitionSpec as P

STEPS = 2
F32 = jnp.float32
BF16 = jnp.bfloat16
MESH = pl.DeviceIdType.MESH


def mixing_of(m):
    return 0.02 + 0.25 * jnp.abs(m.astype(F32))


def shifted(x, by, axis):
    return pltpu.roll(x, (-by) % x.shape[axis], axis)


def latitude_coeffs(cy):
    lane = lax.broadcasted_iota(jnp.int32, cy.shape, 1)
    north = jnp.where(lane == cy.shape[1] - 1, 0.0, shifted(jnp.maximum(cy, 0.0), 1, 1))
    south = jnp.where(lane == 0, 0.0, shifted(-jnp.minimum(cy, 0.0), -1, 1))
    return north, south


def level_coeffs(met, k, levels):
    cx = met(0, k).astype(F32)
    cy = met(1, k).astype(F32)
    below = jnp.maximum(k - 1, 0)
    up = mixing_of(met(2, k)) * (k < levels - 1).astype(F32)
    down = mixing_of(met(2, below)) * (k > 0).astype(F32)
    row = lax.broadcasted_iota(jnp.int32, cx.shape, 0)
    east = jnp.where(row == cx.shape[0] - 1, 0.0, shifted(jnp.maximum(cx, 0.0), 1, 0))
    west = jnp.where(row == 0, 0.0, shifted(-jnp.minimum(cx, 0.0), -1, 0))
    north, south = latitude_coeffs(cy)
    centre = 1.0 - jnp.abs(cx) - jnp.abs(cy) - up - down
    return centre, up, down, east, west, north, south


def advance(lam, above, below, coeffs):
    centre, up, down, east, west, north, south = coeffs
    out = lam * centre + (above * up + below * down)
    out += shifted(lam, 1, 0) * east + shifted(lam, -1, 0) * west
    out += shifted(lam, 1, 1) * north + shifted(lam, -1, 1) * south
    return out


def first_step(
    tiles,
    ranks,
    hour_hbm,
    ids_hbm,
    lam_hbm,
    met_hbm,
    forcing_hbm,
    lam1,
    met1_ref,
    halo_ref,
    rows_ref,
    hour_ref,
    ids_ref,
    lam,
    met_ref,
    forcing_ref,
    met0,
    edges,
    lam_out,
    lam_in,
    cx_out,
    cx_in,
    flux_out,
    columns,
    load_sem,
    gsend,
    grecv,
    hsend,
    hrecv,
):
    tracers, levels, lons, _ = lam.shape
    share = levels // ranks
    tile, rank = lax.axis_index("tile"), lax.axis_index("rcpt")
    east, west = lax.rem(tile + 1, tiles), lax.rem(tile + tiles - 1, tiles)
    last = lons - 1

    parts = 4 if tracers % 4 == 0 else 1
    some = tracers // parts
    cuts = [pl.ds(n * some, some) for n in range(parts)]
    pairs = [(hour_hbm, hour_ref), (met_hbm, met_ref), (ids_hbm, ids_ref)]
    pairs += [(lam_hbm.at[cut], lam.at[cut]) for cut in cuts]
    pairs += [(forcing_hbm, forcing_ref)]
    loads = [pltpu.make_async_copy(*pair, load_sem.at[n]) for n, pair in enumerate(pairs)]
    for load in loads:
        load.start()

    bits = []
    b = ranks // 2
    while b:
        bits.append(b)
        b //= 2
    barrier = pltpu.get_barrier_semaphore()
    for other in (east, west):
        pl.semaphore_signal(barrier, inc=1, device_id=(other, rank), device_id_type=MESH)
    for b in bits:
        pl.semaphore_signal(barrier, inc=1, device_id=(tile, rank ^ b), device_id_type=MESH)

    loads[0].wait()
    loads[1].wait()
    mine = pl.ds(rank * share, share)
    met0[:, mine] = met_ref[hour_ref[0]]
    met1_ref[:, mine] = met_ref[hour_ref[1]]

    pl.semaphore_wait(barrier, 2 + len(bits))

    gathers = {}

    def send_block(step, offset, b):
        buf = (met0, met1_ref)[step]
        where = pl.ds((rank ^ offset) * share, share)
        copy = pltpu.make_async_remote_copy(
            src_ref=buf.at[:, where],
            dst_ref=buf.at[:, where],
            send_sem=gsend.at[step, offset ^ b],
            recv_sem=grecv.at[step, offset ^ b],
            device_id=(tile, rank ^ b),
            device_id_type=MESH,
        )
        copy.start()
        gathers[step, offset ^ b] = copy

    def arrived(step, offset):
        buf = (met0, met1_ref)[step]
        where = pl.ds((rank ^ offset) * share, share)
        pltpu.make_async_remote_copy(
            src_ref=buf.at[:, where],
            dst_ref=buf.at[:, where],
            send_sem=gsend.at[step, offset],
            recv_sem=grecv.at[step, offset],
            device_id=(tile, rank ^ offset),
            device_id_type=MESH,
        ).wait_recv()

    def spread(step, offset, after):
        for i in range(after, len(bits)):
            send_block(step, offset, bits[i])

    def forward(step, which):
        for offset in which:
            arrived(step, offset)
            low = offset & -offset
            spread(step, offset, bits.index(low) + 1)

    order = sorted(range(1, ranks), key=lambda o: (bin(o).count("1"), -o))
    passed_on = [o for o in order if o % 2 == 0]
    kept = [o for o in order if o % 2]

    spread(0, 0, 0)

    def pick(t, _):
        for n, c in enumerate((0, 1, last - 1, last)):
            edges[n, t] = lam[t, :, c, :]
        lam_out[0, t] = edges[0, t].astype(BF16)
        lam_out[1, t] = edges[3, t].astype(BF16)
        return 0

    for n in range(parts):
        loads[3 + n].wait()
        lax.fori_loop(n * some, (n + 1) * some, pick, 0, unroll=True)

    def halo_copy(n, src, dst, side):
        return pltpu.make_async_remote_copy(
            src_ref=src.at[side],
            dst_ref=dst.at[side],
            send_sem=hsend.at[n, side],
            recv_sem=hrecv.at[n, side],
            device_id=((west, east)[side], rank),
            device_id_type=MESH,
        )

    lam_copies = [halo_copy(0, lam_out, lam_in, side) for side in (0, 1)]
    for c in lam_copies:
        c.start()

    loads[2].wait()
    loads[-1].wait()

    def source(t, _):
        rows_ref[t] = forcing_ref[ids_ref[t]]
        return 0

    lax.fori_loop(0, tracers, source, 0, unroll=True)

    forward(0, order)
    spread(1, 0, 0)

    def pick_met(k, _):
        cx = met0[0, k].astype(F32)
        cy = met0[1, k].astype(F32)
        kz = met0[2, k].astype(F32)
        rows = [cx[0:1], cx[1:2], cx[last - 1 : last], cx[last : last + 1]]
        rows += [cy[0:1], cy[last : last + 1], kz[0:1], kz[last : last + 1]]
        for n, r in enumerate(rows):
            columns[n, pl.ds(k, 1), :] = r
        return 0

    lax.fori_loop(0, levels, pick_met, 0, unroll=True)
    cx_out[0] = columns[0].astype(BF16)
    cx_out[1] = columns[3].astype(BF16)
    cx_copies = [halo_copy(1, cx_out, cx_in, side) for side in (0, 1)]
    for c in cx_copies:
        c.start()

    def level(k, _):
        coeffs = level_coeffs(lambda f, n: met0[f, n], k, levels)
        above = jnp.minimum(k + 1, levels - 1)
        below = jnp.maximum(k - 1, 0)

        def one(t, _):
            lam1[t, k] = advance(lam[t, k], lam[t, above], lam[t, below], coeffs)
            return 0

        lax.fori_loop(0, tracers, one, 0, unroll=True)
        return 0

    lax.fori_loop(0, levels // 2, level, 0)
    forward(1, passed_on)
    lax.fori_loop(levels // 2, levels, level, 0)

    def add_rows(t, _):
        lam1[t, levels - 1] += rows_ref[t].astype(F32)
        return 0

    lax.fori_loop(0, tracers, add_rows, 0, unroll=True)

    forward(1, kept)

    def pick_next(k, _):
        cx = met1_ref[0, k].astype(F32)
        columns[8, pl.ds(k, 1), :] = cx[0:1]
        columns[9, pl.ds(k, 1), :] = cx[last : last + 1]
        return 0

    lax.fori_loop(0, levels, pick_next, 0, unroll=True)

    for c in cx_copies + lam_copies:
        c.wait()

    def edge_coeffs(side):
        cx = columns[(0, 3)[side]]
        cy = columns[4 + side]
        kz = mixing_of(columns[6 + side])
        row = lax.broadcasted_iota(jnp.int32, kz.shape, 0)
        up = jnp.where(row == levels - 1, 0.0, kz)
        down = shifted(up, -1, 0)
        north, south = latitude_coeffs(cy)
        if side == 0:
            from_east = jnp.maximum(columns[1], 0.0)
            from_west = -jnp.minimum(cx_in[1].astype(F32), 0.0)
            leaves = jnp.maximum(columns[8], 0.0)
        else:
            from_east = jnp.maximum(cx_in[0].astype(F32), 0.0)
            from_west = -jnp.minimum(columns[2], 0.0)
            leaves = -jnp.minimum(columns[9], 0.0)
        centre = 1.0 - jnp.abs(cx) - jnp.abs(cy) - up - down
        return centre, up, down, from_east, from_west, north, south, leaves

    flux_copies = []
    for side in (0, 1):
        centre, up, down, from_east, from_west, north, south, leaves = edge_coeffs(side)
        top = lax.broadcasted_iota(jnp.int32, centre.shape, 0) == levels - 1
        c = (0, last)[side]

        def edge(t, _):
            x = edges[(0, 3)[side], t]
            if side == 0:
                e, w = edges[1, t], lam_in[1, t].astype(F32)
            else:
                e, w = lam_in[0, t].astype(F32), edges[2, t]
            out = x * centre + shifted(x, 1, 0) * up + shifted(x, -1, 0) * down
            out += e * from_east + w * from_west
            out += shifted(x, 1, 1) * north + shifted(x, -1, 1) * south
            out += jnp.where(top, rows_ref[t].astype(F32)[c : c + 1], 0.0)
            flux_out[side, t] = (out * leaves).astype(BF16)
            lam1[t, :, c, :] = out
            return 0

        lax.fori_loop(0, tracers, edge, 0, unroll=True)
        copy = halo_copy(2, flux_out, halo_ref, side)
        copy.start()
        flux_copies.append(copy)

    for copy in gathers.values():
        copy.wait_send()
    for copy in flux_copies:
        copy.wait()


def second_step(lam_ref, met_ref, halo_ref, rows_ref, out_ref, halo):
    tracers, levels, lons, _ = lam_ref.shape
    held = out_ref.shape[1]
    step = pl.program_id(0)

    @pl.when(step == 0)
    def _():
        halo[...] = halo_ref[...].astype(F32)

    row = lax.broadcasted_iota(jnp.int32, lam_ref.shape[2:], 0)

    def level(n, _):
        k = step * held + n
        coeffs = level_coeffs(lambda f, m: met_ref[f, m], k, levels)
        above = jnp.minimum(k + 1, levels - 1)
        below = jnp.maximum(k - 1, 0)
        for t in range(tracers):
            out = advance(lam_ref[t, k], lam_ref[t, above], lam_ref[t, below], coeffs)
            out += jnp.where(row == lons - 1, halo[0, t, pl.ds(k, 1), :], 0.0)
            out += jnp.where(row == 0, halo[1, t, pl.ds(k, 1), :], 0.0)
            out_ref[t, n] = out
        return 0

    lax.fori_loop(0, held, level, 0)

    @pl.when(step == levels // held - 1)
    def _():
        for t in range(tracers):
            out_ref[t, held - 1] += rows_ref[t].astype(F32)


def per_device(tiles, ranks, adjoint_state, met_fields, forcing, cluster_ids, hour_index):
    tracers, levels, lons, lats = adjoint_state.shape
    fields = met_fields.shape[1]
    vmem = pl.BlockSpec(memory_space=pltpu.VMEM)
    hbm = pl.BlockSpec(memory_space=pltpu.HBM)
    both = (2, tracers, levels, lats)
    arrays = (hour_index, cluster_ids, adjoint_state, met_fields, forcing)
    arrays = [pltpu.with_memory_space_constraint(x, pltpu.HBM) for x in arrays]
    lam1, met1, halo, rows = pl.pallas_call(
        functools.partial(first_step, tiles, ranks),
        out_shape=(
            jax.ShapeDtypeStruct(adjoint_state.shape, F32),
            jax.ShapeDtypeStruct((fields, levels, lons, lats), BF16),
            jax.ShapeDtypeStruct(both, BF16),
            jax.ShapeDtypeStruct((tracers, lons, lats), BF16),
        ),
        in_specs=[hbm] * 5,
        out_specs=(vmem,) * 4,
        scratch_shapes=[
            pltpu.SMEM(hour_index.shape, jnp.int32),
            pltpu.SMEM(cluster_ids.shape, jnp.int32),
            pltpu.VMEM(adjoint_state.shape, F32),
            pltpu.VMEM(met_fields.shape, BF16),
            pltpu.VMEM(forcing.shape, BF16),
            pltpu.VMEM((fields, levels, lons, lats), BF16),
            pltpu.VMEM((4, tracers, levels, lats), F32),
            pltpu.VMEM(both, BF16),
            pltpu.VMEM(both, BF16),
            pltpu.VMEM((2, levels, lats), BF16),
            pltpu.VMEM((2, levels, lats), BF16),
            pltpu.VMEM(both, BF16),
            pltpu.VMEM((10, levels, lats), F32),
            pltpu.SemaphoreType.DMA((8,)),
            pltpu.SemaphoreType.DMA((STEPS, ranks)),
            pltpu.SemaphoreType.DMA((STEPS, ranks)),
            pltpu.SemaphoreType.DMA((3, 2)),
            pltpu.SemaphoreType.DMA((3, 2)),
        ],
        compiler_params=pltpu.CompilerParams(
            collective_id=0, has_side_effects=True, vmem_limit_bytes=40 << 20
        ),
        name="first_step",
    )(*arrays)

    held = 4 if levels % 4 == 0 else 1
    return pl.pallas_call(
        second_step,
        grid=(levels // held,),
        out_shape=jax.ShapeDtypeStruct(adjoint_state.shape, F32),
        in_specs=[vmem] * 4,
        out_specs=pl.BlockSpec((tracers, held, lons, lats), lambda k: (0, k, 0, 0)),
        scratch_shapes=[pltpu.VMEM(both, F32)],
        compiler_params=pltpu.CompilerParams(vmem_limit_bytes=40 << 20),
        name="second_step",
    )(lam1, met1, halo, rows)


def solution(mesh):
    placed = (
        P("rcpt", None, "tile", None),
        P(None, None, "rcpt", "tile", None),
        P(None, "tile", None),
        P("rcpt"),
        P(),
    )
    return jax.shard_map(
        functools.partial(per_device, mesh.shape["tile"], mesh.shape["rcpt"]),
        mesh=mesh,
        in_specs=placed,
        out_specs=P("rcpt", None, "tile", None),
        check_vma=False,
    )
```

```python
import functools

import jax
import jax.numpy as jnp
from jax import lax
from jax.experimental import pallas as pl
from jax.experimental.pallas import tpu as pltpu
from jax.sharding import PartitionSpec as P

STEPS = 2
F32 = jnp.float32
BF16 = jnp.bfloat16
MESH = pl.DeviceIdType.MESH


def mixing_of(m):
    return 0.02 + 0.25 * jnp.abs(m.astype(F32))


def shifted(x, by, axis):
    return pltpu.roll(x, (-by) % x.shape[axis], axis)


def latitude_coeffs(cy):
    lane = lax.broadcasted_iota(jnp.int32, cy.shape, 1)
    north = jnp.where(lane == cy.shape[1] - 1, 0.0, shifted(jnp.maximum(cy, 0.0), 1, 1))
    south = jnp.where(lane == 0, 0.0, shifted(-jnp.minimum(cy, 0.0), -1, 1))
    return north, south


def level_coeffs(met, k, levels):
    cx = met(0, k).astype(F32)
    cy = met(1, k).astype(F32)
    below = jnp.maximum(k - 1, 0)
    up = mixing_of(met(2, k)) * (k < levels - 1).astype(F32)
    down = mixing_of(met(2, below)) * (k > 0).astype(F32)
    row = lax.broadcasted_iota(jnp.int32, cx.shape, 0)
    east = jnp.where(row == cx.shape[0] - 1, 0.0, shifted(jnp.maximum(cx, 0.0), 1, 0))
    west = jnp.where(row == 0, 0.0, shifted(-jnp.minimum(cx, 0.0), -1, 0))
    north, south = latitude_coeffs(cy)
    centre = 1.0 - jnp.abs(cx) - jnp.abs(cy) - up - down
    return centre, up, down, east, west, north, south


def advance(lam, above, below, coeffs):
    centre, up, down, east, west, north, south = coeffs
    out = lam * centre + (above * up + below * down)
    out += shifted(lam, 1, 0) * east + shifted(lam, -1, 0) * west
    out += shifted(lam, 1, 1) * north + shifted(lam, -1, 1) * south
    return out


def both_steps(
    tiles,
    ranks,
    hour_hbm,
    ids_hbm,
    lam_hbm,
    met_hbm,
    forcing_hbm,
    lam2,
    halo_ref,
    met1_ref,
    rows_ref,
    hour_ref,
    ids_ref,
    lam,
    lam1,
    met_ref,
    forcing_ref,
    met0,
    edges,
    lam_out,
    lam_in,
    cx_out,
    cx_in,
    flux_out,
    columns,
    load_sem,
    gsend,
    grecv,
    hsend,
    hrecv,
    fsend,
    frecv,
):
    tracers, levels, lons, _ = lam.shape
    share = levels // ranks
    tile, rank = lax.axis_index("tile"), lax.axis_index("rcpt")
    east, west = lax.rem(tile + 1, tiles), lax.rem(tile + tiles - 1, tiles)
    last = lons - 1

    parts = 4 if tracers % 4 == 0 else 1
    some = tracers // parts
    cuts = [pl.ds(n * some, some) for n in range(parts)]
    pairs = [(hour_hbm, hour_ref), (met_hbm, met_ref), (ids_hbm, ids_ref)]
    pairs += [(lam_hbm.at[cut], lam.at[cut]) for cut in cuts]
    pairs += [(forcing_hbm, forcing_ref)]
    loads = [pltpu.make_async_copy(*pair, load_sem.at[n]) for n, pair in enumerate(pairs)]
    for load in loads:
        load.start()

    bits = []
    b = ranks // 2
    while b:
        bits.append(b)
        b //= 2
    barrier = pltpu.get_barrier_semaphore()
    for other in (east, west):
        pl.semaphore_signal(barrier, inc=1, device_id=(other, rank), device_id_type=MESH)
    for b in bits:
        pl.semaphore_signal(barrier, inc=1, device_id=(tile, rank ^ b), device_id_type=MESH)

    loads[0].wait()
    loads[1].wait()
    mine = pl.ds(rank * share, share)
    met0[:, mine] = met_ref[hour_ref[0]]
    met1_ref[:, mine] = met_ref[hour_ref[1]]

    pl.semaphore_wait(barrier, 2 + len(bits))

    gathers = {}

    def send_block(step, offset, b):
        buf = (met0, met1_ref)[step]
        where = pl.ds((rank ^ offset) * share, share)
        copy = pltpu.make_async_remote_copy(
            src_ref=buf.at[:, where],
            dst_ref=buf.at[:, where],
            send_sem=gsend.at[step, offset ^ b],
            recv_sem=grecv.at[step, offset ^ b],
            device_id=(tile, rank ^ b),
            device_id_type=MESH,
        )
        copy.start()
        gathers[step, offset ^ b] = copy

    def arrived(step, offset):
        buf = (met0, met1_ref)[step]
        where = pl.ds((rank ^ offset) * share, share)
        pltpu.make_async_remote_copy(
            src_ref=buf.at[:, where],
            dst_ref=buf.at[:, where],
            send_sem=gsend.at[step, offset],
            recv_sem=grecv.at[step, offset],
            device_id=(tile, rank ^ offset),
            device_id_type=MESH,
        ).wait_recv()

    def spread(step, offset, after):
        for i in range(after, len(bits)):
            send_block(step, offset, bits[i])

    def forward(step, which):
        for offset in which:
            arrived(step, offset)
            low = offset & -offset
            spread(step, offset, bits.index(low) + 1)

    order = sorted(range(1, ranks), key=lambda o: (bin(o).count("1"), -o))
    passed_on = [o for o in order if o % 2 == 0]
    kept = [o for o in order if o % 2]

    spread(0, 0, 0)

    def pick(t, _):
        for n, c in enumerate((0, 1, last - 1, last)):
            edges[n, t] = lam[t, :, c, :]
        lam_out[0, t] = edges[0, t].astype(BF16)
        lam_out[1, t] = edges[3, t].astype(BF16)
        return 0

    for n in range(parts):
        loads[3 + n].wait()
        lax.fori_loop(n * some, (n + 1) * some, pick, 0, unroll=True)

    def halo_copy(n, src, dst, side):
        return pltpu.make_async_remote_copy(
            src_ref=src.at[side],
            dst_ref=dst.at[side],
            send_sem=hsend.at[n, side],
            recv_sem=hrecv.at[n, side],
            device_id=((west, east)[side], rank),
            device_id_type=MESH,
        )

    lam_copies = [halo_copy(0, lam_out, lam_in, side) for side in (0, 1)]
    for c in lam_copies:
        c.start()

    loads[2].wait()
    loads[-1].wait()

    def source(t, _):
        rows_ref[t] = forcing_ref[ids_ref[t]]
        return 0

    lax.fori_loop(0, tracers, source, 0, unroll=True)

    forward(0, order)
    spread(1, 0, 0)

    def pick_met(k, _):
        cx = met0[0, k].astype(F32)
        cy = met0[1, k].astype(F32)
        kz = met0[2, k].astype(F32)
        rows = [cx[0:1], cx[1:2], cx[last - 1 : last], cx[last : last + 1]]
        rows += [cy[0:1], cy[last : last + 1], kz[0:1], kz[last : last + 1]]
        for n, r in enumerate(rows):
            columns[n, pl.ds(k, 1), :] = r
        return 0

    lax.fori_loop(0, levels, pick_met, 0, unroll=True)
    cx_out[0] = columns[0].astype(BF16)
    cx_out[1] = columns[3].astype(BF16)
    cx_copies = [halo_copy(1, cx_out, cx_in, side) for side in (0, 1)]
    for c in cx_copies:
        c.start()

    def run_levels(first, end, new, old, met):
        def level(k, _):
            coeffs = level_coeffs(lambda f, n: met[f, n], k, levels)
            above = jnp.minimum(k + 1, levels - 1)
            below = jnp.maximum(k - 1, 0)

            def one(t, _):
                new[t, k] = advance(old[t, k], old[t, above], old[t, below], coeffs)
                return 0

            lax.fori_loop(0, tracers, one, 0, unroll=True)
            return 0

        lax.fori_loop(first, end, level, 0)

    def add_rows(new):
        def one(t, _):
            new[t, levels - 1] += rows_ref[t].astype(F32)
            return 0

        lax.fori_loop(0, tracers, one, 0, unroll=True)

    run_levels(0, levels // 2, lam1, lam, met0)
    forward(1, passed_on)
    run_levels(levels // 2, levels, lam1, lam, met0)
    add_rows(lam1)
    forward(1, kept)

    def pick_next(k, _):
        cx = met1_ref[0, k].astype(F32)
        columns[8, pl.ds(k, 1), :] = cx[0:1]
        columns[9, pl.ds(k, 1), :] = cx[last : last + 1]
        return 0

    lax.fori_loop(0, levels, pick_next, 0, unroll=True)

    for c in cx_copies + lam_copies:
        c.wait()

    def edge_coeffs(side):
        cx = columns[(0, 3)[side]]
        cy = columns[4 + side]
        kz = mixing_of(columns[6 + side])
        row = lax.broadcasted_iota(jnp.int32, kz.shape, 0)
        up = jnp.where(row == levels - 1, 0.0, kz)
        down = shifted(up, -1, 0)
        north, south = latitude_coeffs(cy)
        if side == 0:
            from_east = jnp.maximum(columns[1], 0.0)
            from_west = -jnp.minimum(cx_in[1].astype(F32), 0.0)
            leaves = jnp.maximum(columns[8], 0.0)
        else:
            from_east = jnp.maximum(cx_in[0].astype(F32), 0.0)
            from_west = -jnp.minimum(columns[2], 0.0)
            leaves = -jnp.minimum(columns[9], 0.0)
        centre = 1.0 - jnp.abs(cx) - jnp.abs(cy) - up - down
        return centre, up, down, from_east, from_west, north, south, leaves

    def flux_copy(side, part):
        cut = pl.ds(part * half, half)
        return pltpu.make_async_remote_copy(
            src_ref=flux_out.at[side, cut],
            dst_ref=halo_ref.at[side, cut],
            send_sem=fsend.at[side, part],
            recv_sem=frecv.at[side, part],
            device_id=((west, east)[side], rank),
            device_id_type=MESH,
        )

    halves = 2 if tracers % 2 == 0 else 1
    half = tracers // halves
    flux_copies = []
    for side in (0, 1):
        centre, up, down, from_east, from_west, north, south, leaves = edge_coeffs(side)
        top = lax.broadcasted_iota(jnp.int32, centre.shape, 0) == levels - 1
        c = (0, last)[side]

        def edge(t, _):
            x = edges[(0, 3)[side], t]
            if side == 0:
                e, w = edges[1, t], lam_in[1, t].astype(F32)
            else:
                e, w = lam_in[0, t].astype(F32), edges[2, t]
            out = x * centre + shifted(x, 1, 0) * up + shifted(x, -1, 0) * down
            out += e * from_east + w * from_west
            out += shifted(x, 1, 1) * north + shifted(x, -1, 1) * south
            out += jnp.where(top, rows_ref[t].astype(F32)[c : c + 1], 0.0)
            flux_out[side, t] = (out * leaves).astype(BF16)
            lam1[t, :, c, :] = out
            return 0

        for part in range(halves):
            lax.fori_loop(part * half, (part + 1) * half, edge, 0, unroll=True)
            copy = flux_copy(side, part)
            copy.start()
            flux_copies.append(copy)

    run_levels(0, levels, lam2, lam1, met1_ref)
    add_rows(lam2)

    for copy in gathers.values():
        copy.wait_send()
    for copy in flux_copies:
        copy.wait()


def add_halo(lam_ref, halo_ref, out_ref, halo):
    tracers, levels, lons, _ = lam_ref.shape
    held = out_ref.shape[1]
    step = pl.program_id(0)

    @pl.when(step == 0)
    def _():
        halo[...] = halo_ref[...].astype(F32)

    row = lax.broadcasted_iota(jnp.int32, lam_ref.shape[2:], 0)

    def level(n, _):
        k = step * held + n
        for t in range(tracers):
            out = lam_ref[t, k]
            out += jnp.where(row == lons - 1, halo[0, t, pl.ds(k, 1), :], 0.0)
            out += jnp.where(row == 0, halo[1, t, pl.ds(k, 1), :], 0.0)
            out_ref[t, n] = out
        return 0

    lax.fori_loop(0, held, level, 0)


def per_device(tiles, ranks, adjoint_state, met_fields, forcing, cluster_ids, hour_index):
    tracers, levels, lons, lats = adjoint_state.shape
    fields = met_fields.shape[1]
    vmem = pl.BlockSpec(memory_space=pltpu.VMEM)
    hbm = pl.BlockSpec(memory_space=pltpu.HBM)
    both = (2, tracers, levels, lats)
    arrays = (hour_index, cluster_ids, adjoint_state, met_fields, forcing)
    arrays = [pltpu.with_memory_space_constraint(x, pltpu.HBM) for x in arrays]
    lam2, halo = pl.pallas_call(
        functools.partial(both_steps, tiles, ranks),
        out_shape=(
            jax.ShapeDtypeStruct(adjoint_state.shape, F32),
            jax.ShapeDtypeStruct(both, BF16),
        ),
        in_specs=[hbm] * 5,
        out_specs=(vmem,) * 2,
        scratch_shapes=[
            pltpu.VMEM((fields, levels, lons, lats), BF16),
            pltpu.VMEM((tracers, lons, lats), BF16),
            pltpu.SMEM(hour_index.shape, jnp.int32),
            pltpu.SMEM(cluster_ids.shape, jnp.int32),
            pltpu.VMEM(adjoint_state.shape, F32),
            pltpu.VMEM(adjoint_state.shape, F32),
            pltpu.VMEM(met_fields.shape, BF16),
            pltpu.VMEM(forcing.shape, BF16),
            pltpu.VMEM((fields, levels, lons, lats), BF16),
            pltpu.VMEM((4, tracers, levels, lats), F32),
            pltpu.VMEM(both, BF16),
            pltpu.VMEM(both, BF16),
            pltpu.VMEM((2, levels, lats), BF16),
            pltpu.VMEM((2, levels, lats), BF16),
            pltpu.VMEM(both, BF16),
            pltpu.VMEM((10, levels, lats), F32),
            pltpu.SemaphoreType.DMA((8,)),
            pltpu.SemaphoreType.DMA((STEPS, ranks)),
            pltpu.SemaphoreType.DMA((STEPS, ranks)),
            pltpu.SemaphoreType.DMA((2, 2)),
            pltpu.SemaphoreType.DMA((2, 2)),
            pltpu.SemaphoreType.DMA((2, 2)),
            pltpu.SemaphoreType.DMA((2, 2)),
        ],
        compiler_params=pltpu.CompilerParams(
            collective_id=0, has_side_effects=True, vmem_limit_bytes=40 << 20
        ),
        name="both_steps",
    )(*arrays)

    held = 4 if levels % 4 == 0 else 1
    return pl.pallas_call(
        add_halo,
        grid=(levels // held,),
        out_shape=jax.ShapeDtypeStruct(adjoint_state.shape, F32),
        in_specs=[vmem] * 2,
        out_specs=pl.BlockSpec((tracers, held, lons, lats), lambda k: (0, k, 0, 0)),
        scratch_shapes=[pltpu.VMEM(both, F32)],
        compiler_params=pltpu.CompilerParams(vmem_limit_bytes=40 << 20),
        name="add_halo",
    )(lam2, halo)


def solution(mesh):
    placed = (
        P("rcpt", None, "tile", None),
        P(None, None, "rcpt", "tile", None),
        P(None, "tile", None),
        P("rcpt"),
        P(),
    )
    return jax.shard_map(
        functools.partial(per_device, mesh.shape["tile"], mesh.shape["rcpt"]),
        mesh=mesh,
        in_specs=placed,
        out_specs=P("rcpt", None, "tile", None),
        check_vma=False,
    )
```

```python
import functools

import jax
import jax.numpy as jnp
from jax import lax
from jax.experimental import pallas as pl
from jax.experimental.pallas import tpu as pltpu
from jax.sharding import PartitionSpec as P

STEPS = 2
F32 = jnp.float32
BF16 = jnp.bfloat16
MESH = pl.DeviceIdType.MESH


def mixing_of(m):
    return 0.02 + 0.25 * jnp.abs(m.astype(F32))


def shifted(x, by, axis):
    return pltpu.roll(x, (-by) % x.shape[axis], axis)


def latitude_coeffs(cy):
    lane = lax.broadcasted_iota(jnp.int32, cy.shape, 1)
    north = jnp.where(lane == cy.shape[1] - 1, 0.0, shifted(jnp.maximum(cy, 0.0), 1, 1))
    south = jnp.where(lane == 0, 0.0, shifted(-jnp.minimum(cy, 0.0), -1, 1))
    return north, south


def level_coeffs(met, k, levels):
    cx = met(0, k).astype(F32)
    cy = met(1, k).astype(F32)
    below = jnp.maximum(k - 1, 0)
    up = mixing_of(met(2, k)) * (k < levels - 1).astype(F32)
    down = mixing_of(met(2, below)) * (k > 0).astype(F32)
    row = lax.broadcasted_iota(jnp.int32, cx.shape, 0)
    east = jnp.where(row == cx.shape[0] - 1, 0.0, shifted(jnp.maximum(cx, 0.0), 1, 0))
    west = jnp.where(row == 0, 0.0, shifted(-jnp.minimum(cx, 0.0), -1, 0))
    north, south = latitude_coeffs(cy)
    centre = 1.0 - jnp.abs(cx) - jnp.abs(cy) - up - down
    return centre, up, down, east, west, north, south


def advance(lam, above, below, coeffs):
    centre, up, down, east, west, north, south = coeffs
    out = lam * centre + (above * up + below * down)
    out += shifted(lam, 1, 0) * east + shifted(lam, -1, 0) * west
    out += shifted(lam, 1, 1) * north + shifted(lam, -1, 1) * south
    return out


def both_steps(
    tiles,
    ranks,
    hour_hbm,
    ids_hbm,
    lam_hbm,
    met_hbm,
    forcing_hbm,
    lam2,
    halo_ref,
    met1_ref,
    rows_ref,
    hour_ref,
    ids_ref,
    lam,
    lam1,
    met_ref,
    forcing_ref,
    met0,
    edges,
    lam_out,
    lam_in,
    cx_out,
    cx_in,
    flux_out,
    columns,
    load_sem,
    gsend,
    grecv,
    hsend,
    hrecv,
    fsend,
    frecv,
):
    tracers, levels, lons, _ = lam.shape
    share = levels // ranks
    tile, rank = lax.axis_index("tile"), lax.axis_index("rcpt")
    east, west = lax.rem(tile + 1, tiles), lax.rem(tile + tiles - 1, tiles)
    last = lons - 1

    parts = 4 if tracers % 4 == 0 else 1
    some = tracers // parts
    cuts = [pl.ds(n * some, some) for n in range(parts)]
    pairs = [(hour_hbm, hour_ref), (met_hbm, met_ref), (ids_hbm, ids_ref)]
    pairs += [(lam_hbm.at[cut], lam.at[cut]) for cut in cuts]
    pairs += [(forcing_hbm, forcing_ref)]
    loads = [pltpu.make_async_copy(*pair, load_sem.at[n]) for n, pair in enumerate(pairs)]
    for load in loads:
        load.start()

    bits = []
    b = ranks // 2
    while b:
        bits.append(b)
        b //= 2
    barrier = pltpu.get_barrier_semaphore()
    for other in (east, west):
        pl.semaphore_signal(barrier, inc=1, device_id=(other, rank), device_id_type=MESH)
    for b in bits:
        pl.semaphore_signal(barrier, inc=1, device_id=(tile, rank ^ b), device_id_type=MESH)

    loads[0].wait()
    loads[1].wait()
    mine = pl.ds(rank * share, share)
    met0[:, mine] = met_ref[hour_ref[0]]
    met1_ref[:, mine] = met_ref[hour_ref[1]]

    pl.semaphore_wait(barrier, 2 + len(bits))

    gathers = {}

    def send_block(step, offset, b):
        buf = (met0, met1_ref)[step]
        where = pl.ds((rank ^ offset) * share, share)
        copy = pltpu.make_async_remote_copy(
            src_ref=buf.at[:, where],
            dst_ref=buf.at[:, where],
            send_sem=gsend.at[step, offset ^ b],
            recv_sem=grecv.at[step, offset ^ b],
            device_id=(tile, rank ^ b),
            device_id_type=MESH,
        )
        copy.start()
        gathers[step, offset ^ b] = copy

    def arrived(step, offset):
        buf = (met0, met1_ref)[step]
        where = pl.ds((rank ^ offset) * share, share)
        pltpu.make_async_remote_copy(
            src_ref=buf.at[:, where],
            dst_ref=buf.at[:, where],
            send_sem=gsend.at[step, offset],
            recv_sem=grecv.at[step, offset],
            device_id=(tile, rank ^ offset),
            device_id_type=MESH,
        ).wait_recv()

    def spread(step, offset, after):
        for i in range(after, len(bits)):
            send_block(step, offset, bits[i])

    def forward(step, which):
        for offset in which:
            arrived(step, offset)
            low = offset & -offset
            spread(step, offset, bits.index(low) + 1)

    order = sorted(range(1, ranks), key=lambda o: (bin(o).count("1"), -o))
    passed_on = [o for o in order if o % 2 == 0]
    kept = [o for o in order if o % 2]

    spread(0, 0, 0)

    def pick(t, _):
        for n, c in enumerate((0, 1, last - 1, last)):
            edges[n, t] = lam[t, :, c, :]
        lam_out[0, t] = edges[0, t].astype(BF16)
        lam_out[1, t] = edges[3, t].astype(BF16)
        return 0

    for n in range(parts):
        loads[3 + n].wait()
        lax.fori_loop(n * some, (n + 1) * some, pick, 0, unroll=True)

    def halo_copy(n, src, dst, side):
        return pltpu.make_async_remote_copy(
            src_ref=src.at[side],
            dst_ref=dst.at[side],
            send_sem=hsend.at[n, side],
            recv_sem=hrecv.at[n, side],
            device_id=((west, east)[side], rank),
            device_id_type=MESH,
        )

    lam_copies = [halo_copy(0, lam_out, lam_in, side) for side in (0, 1)]
    for c in lam_copies:
        c.start()

    loads[2].wait()
    loads[-1].wait()

    def source(t, _):
        rows_ref[t] = forcing_ref[ids_ref[t]]
        return 0

    lax.fori_loop(0, tracers, source, 0, unroll=True)

    forward(0, order)
    spread(1, 0, 0)

    def pick_met(k, _):
        cx = met0[0, k].astype(F32)
        cy = met0[1, k].astype(F32)
        kz = met0[2, k].astype(F32)
        rows = [cx[0:1], cx[1:2], cx[last - 1 : last], cx[last : last + 1]]
        rows += [cy[0:1], cy[last : last + 1], kz[0:1], kz[last : last + 1]]
        for n, r in enumerate(rows):
            columns[n, pl.ds(k, 1), :] = r
        return 0

    lax.fori_loop(0, levels, pick_met, 0, unroll=True)
    cx_out[0] = columns[0].astype(BF16)
    cx_out[1] = columns[3].astype(BF16)
    cx_copies = [halo_copy(1, cx_out, cx_in, side) for side in (0, 1)]
    for c in cx_copies:
        c.start()

    def run_levels(first, end, new, old, met):
        def level(k, _):
            coeffs = level_coeffs(lambda f, n: met[f, n], k, levels)
            above = jnp.minimum(k + 1, levels - 1)
            below = jnp.maximum(k - 1, 0)

            def one(t, _):
                new[t, k] = advance(old[t, k], old[t, above], old[t, below], coeffs)
                return 0

            lax.fori_loop(0, tracers, one, 0, unroll=True)
            return 0

        lax.fori_loop(first, end, level, 0)

    def add_rows(new):
        def one(t, _):
            new[t, levels - 1] += rows_ref[t].astype(F32)
            return 0

        lax.fori_loop(0, tracers, one, 0, unroll=True)

    run_levels(0, levels // 4, lam1, lam, met0)
    forward(1, passed_on)
    run_levels(levels // 4, levels // 2, lam1, lam, met0)
    forward(1, kept)

    def pick_next(k, _):
        cx = met1_ref[0, k].astype(F32)
        columns[8, pl.ds(k, 1), :] = cx[0:1]
        columns[9, pl.ds(k, 1), :] = cx[last : last + 1]
        return 0

    lax.fori_loop(0, levels, pick_next, 0, unroll=True)

    for c in cx_copies + lam_copies:
        c.wait()

    def edge_coeffs(side):
        cx = columns[(0, 3)[side]]
        cy = columns[4 + side]
        kz = mixing_of(columns[6 + side])
        row = lax.broadcasted_iota(jnp.int32, kz.shape, 0)
        up = jnp.where(row == levels - 1, 0.0, kz)
        down = shifted(up, -1, 0)
        north, south = latitude_coeffs(cy)
        if side == 0:
            from_east = jnp.maximum(columns[1], 0.0)
            from_west = -jnp.minimum(cx_in[1].astype(F32), 0.0)
            leaves = jnp.maximum(columns[8], 0.0)
        else:
            from_east = jnp.maximum(cx_in[0].astype(F32), 0.0)
            from_west = -jnp.minimum(columns[2], 0.0)
            leaves = -jnp.minimum(columns[9], 0.0)
        centre = 1.0 - jnp.abs(cx) - jnp.abs(cy) - up - down
        return centre, up, down, from_east, from_west, north, south, leaves

    def flux_copy(side, part):
        cut = pl.ds(part * half, half)
        return pltpu.make_async_remote_copy(
            src_ref=flux_out.at[side, cut],
            dst_ref=halo_ref.at[side, cut],
            send_sem=fsend.at[side, part],
            recv_sem=frecv.at[side, part],
            device_id=((west, east)[side], rank),
            device_id_type=MESH,
        )

    halves = 2 if tracers % 2 == 0 else 1
    half = tracers // halves
    flux_copies = []
    for side in (0, 1):
        centre, up, down, from_east, from_west, north, south, leaves = edge_coeffs(side)
        top = lax.broadcasted_iota(jnp.int32, centre.shape, 0) == levels - 1
        c = (0, last)[side]

        def edge(t, _):
            x = edges[(0, 3)[side], t]
            if side == 0:
                e, w = edges[1, t], lam_in[1, t].astype(F32)
            else:
                e, w = lam_in[0, t].astype(F32), edges[2, t]
            out = x * centre + shifted(x, 1, 0) * up + shifted(x, -1, 0) * down
            out += e * from_east + w * from_west
            out += shifted(x, 1, 1) * north + shifted(x, -1, 1) * south
            out += jnp.where(top, rows_ref[t].astype(F32)[c : c + 1], 0.0)
            flux_out[side, t] = (out * leaves).astype(BF16)
            edges[(0, 3)[side], t] = out
            return 0

        for part in range(halves):
            lax.fori_loop(part * half, (part + 1) * half, edge, 0, unroll=True)
            copy = flux_copy(side, part)
            copy.start()
            flux_copies.append(copy)

    run_levels(levels // 2, levels, lam1, lam, met0)
    add_rows(lam1)

    def put(t, _):
        lam1[t, :, 0, :] = edges[0, t]
        lam1[t, :, last, :] = edges[3, t]
        return 0

    lax.fori_loop(0, tracers, put, 0, unroll=True)

    run_levels(0, levels, lam2, lam1, met1_ref)
    add_rows(lam2)

    for copy in gathers.values():
        copy.wait_send()
    for copy in flux_copies:
        copy.wait()


def add_halo(lam_ref, halo_ref, out_ref, halo):
    tracers, levels, lons, _ = lam_ref.shape
    held = out_ref.shape[1]
    step = pl.program_id(0)

    @pl.when(step == 0)
    def _():
        halo[...] = halo_ref[...].astype(F32)

    row = lax.broadcasted_iota(jnp.int32, lam_ref.shape[2:], 0)

    def level(n, _):
        k = step * held + n
        for t in range(tracers):
            out = lam_ref[t, k]
            out += jnp.where(row == lons - 1, halo[0, t, pl.ds(k, 1), :], 0.0)
            out += jnp.where(row == 0, halo[1, t, pl.ds(k, 1), :], 0.0)
            out_ref[t, n] = out
        return 0

    lax.fori_loop(0, held, level, 0)


def per_device(tiles, ranks, adjoint_state, met_fields, forcing, cluster_ids, hour_index):
    tracers, levels, lons, lats = adjoint_state.shape
    fields = met_fields.shape[1]
    vmem = pl.BlockSpec(memory_space=pltpu.VMEM)
    hbm = pl.BlockSpec(memory_space=pltpu.HBM)
    both = (2, tracers, levels, lats)
    arrays = (hour_index, cluster_ids, adjoint_state, met_fields, forcing)
    arrays = [pltpu.with_memory_space_constraint(x, pltpu.HBM) for x in arrays]
    lam2, halo = pl.pallas_call(
        functools.partial(both_steps, tiles, ranks),
        out_shape=(
            jax.ShapeDtypeStruct(adjoint_state.shape, F32),
            jax.ShapeDtypeStruct(both, BF16),
        ),
        in_specs=[hbm] * 5,
        out_specs=(vmem,) * 2,
        scratch_shapes=[
            pltpu.VMEM((fields, levels, lons, lats), BF16),
            pltpu.VMEM((tracers, lons, lats), BF16),
            pltpu.SMEM(hour_index.shape, jnp.int32),
            pltpu.SMEM(cluster_ids.shape, jnp.int32),
            pltpu.VMEM(adjoint_state.shape, F32),
            pltpu.VMEM(adjoint_state.shape, F32),
            pltpu.VMEM(met_fields.shape, BF16),
            pltpu.VMEM(forcing.shape, BF16),
            pltpu.VMEM((fields, levels, lons, lats), BF16),
            pltpu.VMEM((4, tracers, levels, lats), F32),
            pltpu.VMEM(both, BF16),
            pltpu.VMEM(both, BF16),
            pltpu.VMEM((2, levels, lats), BF16),
            pltpu.VMEM((2, levels, lats), BF16),
            pltpu.VMEM(both, BF16),
            pltpu.VMEM((10, levels, lats), F32),
            pltpu.SemaphoreType.DMA((8,)),
            pltpu.SemaphoreType.DMA((STEPS, ranks)),
            pltpu.SemaphoreType.DMA((STEPS, ranks)),
            pltpu.SemaphoreType.DMA((2, 2)),
            pltpu.SemaphoreType.DMA((2, 2)),
            pltpu.SemaphoreType.DMA((2, 2)),
            pltpu.SemaphoreType.DMA((2, 2)),
        ],
        compiler_params=pltpu.CompilerParams(
            collective_id=0, has_side_effects=True, vmem_limit_bytes=40 << 20
        ),
        name="both_steps",
    )(*arrays)

    held = 4 if levels % 4 == 0 else 1
    return pl.pallas_call(
        add_halo,
        grid=(levels // held,),
        out_shape=jax.ShapeDtypeStruct(adjoint_state.shape, F32),
        in_specs=[vmem] * 2,
        out_specs=pl.BlockSpec((tracers, held, lons, lats), lambda k: (0, k, 0, 0)),
        scratch_shapes=[pltpu.VMEM(both, F32)],
        compiler_params=pltpu.CompilerParams(vmem_limit_bytes=40 << 20),
        name="add_halo",
    )(lam2, halo)


def solution(mesh):
    placed = (
        P("rcpt", None, "tile", None),
        P(None, None, "rcpt", "tile", None),
        P(None, "tile", None),
        P("rcpt"),
        P(),
    )
    return jax.shard_map(
        functools.partial(per_device, mesh.shape["tile"], mesh.shape["rcpt"]),
        mesh=mesh,
        in_specs=placed,
        out_specs=P("rcpt", None, "tile", None),
        check_vma=False,
    )
```

```python
import functools

import jax
import jax.numpy as jnp
from jax import lax
from jax.experimental import pallas as pl
from jax.experimental.pallas import tpu as pltpu
from jax.sharding import PartitionSpec as P

STEPS = 2
F32 = jnp.float32
BF16 = jnp.bfloat16
MESH = pl.DeviceIdType.MESH


def mixing_of(m):
    return 0.02 + 0.25 * jnp.abs(m.astype(F32))


def shifted(x, by, axis):
    return pltpu.roll(x, (-by) % x.shape[axis], axis)


def latitude_coeffs(cy):
    lane = lax.broadcasted_iota(jnp.int32, cy.shape, 1)
    north = jnp.where(lane == cy.shape[1] - 1, 0.0, shifted(jnp.maximum(cy, 0.0), 1, 1))
    south = jnp.where(lane == 0, 0.0, shifted(-jnp.minimum(cy, 0.0), -1, 1))
    return north, south


def level_coeffs(met, k, levels):
    cx = met(0, k).astype(F32)
    cy = met(1, k).astype(F32)
    below = jnp.maximum(k - 1, 0)
    up = mixing_of(met(2, k)) * (k < levels - 1).astype(F32)
    down = mixing_of(met(2, below)) * (k > 0).astype(F32)
    row = lax.broadcasted_iota(jnp.int32, cx.shape, 0)
    east = jnp.where(row == cx.shape[0] - 1, 0.0, shifted(jnp.maximum(cx, 0.0), 1, 0))
    west = jnp.where(row == 0, 0.0, shifted(-jnp.minimum(cx, 0.0), -1, 0))
    north, south = latitude_coeffs(cy)
    centre = 1.0 - jnp.abs(cx) - jnp.abs(cy) - up - down
    return centre, up, down, east, west, north, south


def advance(lam, above, below, coeffs):
    centre, up, down, east, west, north, south = coeffs
    out = lam * centre + (above * up + below * down)
    out += shifted(lam, 1, 0) * east + shifted(lam, -1, 0) * west
    out += shifted(lam, 1, 1) * north + shifted(lam, -1, 1) * south
    return out


def both_steps(
    tiles,
    ranks,
    hour_hbm,
    ids_hbm,
    lam_hbm,
    met_hbm,
    forcing_hbm,
    lam2,
    halo_ref,
    met1_ref,
    rows_ref,
    hour_ref,
    ids_ref,
    lam,
    lam1,
    met_ref,
    forcing_ref,
    met0,
    edges,
    lam_out,
    lam_in,
    cx_out,
    cx_in,
    flux_out,
    columns,
    load_sem,
    gsend,
    grecv,
    hsend,
    hrecv,
    fsend,
    frecv,
    lsend,
    lrecv,
):
    tracers, levels, lons, _ = lam.shape
    share = levels // ranks
    tile, rank = lax.axis_index("tile"), lax.axis_index("rcpt")
    east, west = lax.rem(tile + 1, tiles), lax.rem(tile + tiles - 1, tiles)
    last = lons - 1

    parts = 4 if tracers % 4 == 0 else 1
    some = tracers // parts
    cuts = [pl.ds(n * some, some) for n in range(parts)]
    pairs = [(hour_hbm, hour_ref), (met_hbm, met_ref), (ids_hbm, ids_ref)]
    pairs += [(lam_hbm.at[cut], lam.at[cut]) for cut in cuts]
    pairs += [(forcing_hbm, forcing_ref)]
    loads = [pltpu.make_async_copy(*pair, load_sem.at[n]) for n, pair in enumerate(pairs)]
    for load in loads:
        load.start()

    bits = []
    b = ranks // 2
    while b:
        bits.append(b)
        b //= 2
    barrier = pltpu.get_barrier_semaphore()
    for other in (east, west):
        pl.semaphore_signal(barrier, inc=1, device_id=(other, rank), device_id_type=MESH)
    for b in bits:
        pl.semaphore_signal(barrier, inc=1, device_id=(tile, rank ^ b), device_id_type=MESH)

    loads[0].wait()
    loads[1].wait()
    mine = pl.ds(rank * share, share)
    met0[:, mine] = met_ref[hour_ref[0]]
    met1_ref[:, mine] = met_ref[hour_ref[1]]

    pl.semaphore_wait(barrier, 2 + len(bits))

    gathers = {}

    def send_block(step, offset, b):
        buf = (met0, met1_ref)[step]
        where = pl.ds((rank ^ offset) * share, share)
        copy = pltpu.make_async_remote_copy(
            src_ref=buf.at[:, where],
            dst_ref=buf.at[:, where],
            send_sem=gsend.at[step, offset ^ b],
            recv_sem=grecv.at[step, offset ^ b],
            device_id=(tile, rank ^ b),
            device_id_type=MESH,
        )
        copy.start()
        gathers[step, offset ^ b] = copy

    def arrived(step, offset):
        buf = (met0, met1_ref)[step]
        where = pl.ds((rank ^ offset) * share, share)
        pltpu.make_async_remote_copy(
            src_ref=buf.at[:, where],
            dst_ref=buf.at[:, where],
            send_sem=gsend.at[step, offset],
            recv_sem=grecv.at[step, offset],
            device_id=(tile, rank ^ offset),
            device_id_type=MESH,
        ).wait_recv()

    def spread(step, offset, after):
        for i in range(after, len(bits)):
            send_block(step, offset, bits[i])

    def forward(step, which):
        for offset in which:
            arrived(step, offset)
            low = offset & -offset
            spread(step, offset, bits.index(low) + 1)

    order = sorted(range(1, ranks), key=lambda o: (bin(o).count("1"), -o))
    passed_on = [o for o in order if o % 2 == 0]
    kept = [o for o in order if o % 2]

    spread(0, 0, 0)

    def pick(t, _):
        for n, c in enumerate((0, 1, last - 1, last)):
            edges[n, t] = lam[t, :, c, :]
        lam_out[0, t] = edges[0, t].astype(BF16)
        lam_out[1, t] = edges[3, t].astype(BF16)
        return 0

    def lam_copy(side, part):
        cut = pl.ds(part * some, some)
        return pltpu.make_async_remote_copy(
            src_ref=lam_out.at[side, cut],
            dst_ref=lam_in.at[side, cut],
            send_sem=lsend.at[side, part],
            recv_sem=lrecv.at[side, part],
            device_id=((west, east)[side], rank),
            device_id_type=MESH,
        )

    lam_copies = []
    for n in range(parts):
        loads[3 + n].wait()
        lax.fori_loop(n * some, (n + 1) * some, pick, 0, unroll=True)
        for side in (0, 1):
            copy = lam_copy(side, n)
            copy.start()
            lam_copies.append(copy)

    def halo_copy(n, src, dst, side):
        return pltpu.make_async_remote_copy(
            src_ref=src.at[side],
            dst_ref=dst.at[side],
            send_sem=hsend.at[n, side],
            recv_sem=hrecv.at[n, side],
            device_id=((west, east)[side], rank),
            device_id_type=MESH,
        )

    loads[2].wait()
    loads[-1].wait()

    def source(t, _):
        rows_ref[t] = forcing_ref[ids_ref[t]]
        return 0

    lax.fori_loop(0, tracers, source, 0, unroll=True)

    forward(0, order)
    spread(1, 0, 0)

    def pick_met(k, _):
        cx = met0[0, k].astype(F32)
        cy = met0[1, k].astype(F32)
        kz = met0[2, k].astype(F32)
        rows = [cx[0:1], cx[1:2], cx[last - 1 : last], cx[last : last + 1]]
        rows += [cy[0:1], cy[last : last + 1], kz[0:1], kz[last : last + 1]]
        for n, r in enumerate(rows):
            columns[n, pl.ds(k, 1), :] = r
        return 0

    lax.fori_loop(0, levels, pick_met, 0, unroll=True)
    cx_out[0] = columns[0].astype(BF16)
    cx_out[1] = columns[3].astype(BF16)
    cx_copies = [halo_copy(1, cx_out, cx_in, side) for side in (0, 1)]
    for c in cx_copies:
        c.start()

    def run_levels(first, end, new, old, met):
        def level(k, _):
            coeffs = level_coeffs(lambda f, n: met[f, n], k, levels)
            above = jnp.minimum(k + 1, levels - 1)
            below = jnp.maximum(k - 1, 0)

            def one(t, _):
                new[t, k] = advance(old[t, k], old[t, above], old[t, below], coeffs)
                return 0

            lax.fori_loop(0, tracers, one, 0, unroll=True)
            return 0

        lax.fori_loop(first, end, level, 0)

    def add_rows(new):
        def one(t, _):
            new[t, levels - 1] += rows_ref[t].astype(F32)
            return 0

        lax.fori_loop(0, tracers, one, 0, unroll=True)

    run_levels(0, levels // 4, lam1, lam, met0)
    forward(1, passed_on)
    run_levels(levels // 4, levels // 2, lam1, lam, met0)
    forward(1, kept)

    def pick_next(k, _):
        cx = met1_ref[0, k].astype(F32)
        columns[8, pl.ds(k, 1), :] = cx[0:1]
        columns[9, pl.ds(k, 1), :] = cx[last : last + 1]
        return 0

    lax.fori_loop(0, levels, pick_next, 0, unroll=True)

    for c in cx_copies + lam_copies:
        c.wait()

    def edge_coeffs(side):
        cx = columns[(0, 3)[side]]
        cy = columns[4 + side]
        kz = mixing_of(columns[6 + side])
        row = lax.broadcasted_iota(jnp.int32, kz.shape, 0)
        up = jnp.where(row == levels - 1, 0.0, kz)
        down = shifted(up, -1, 0)
        north, south = latitude_coeffs(cy)
        if side == 0:
            from_east = jnp.maximum(columns[1], 0.0)
            from_west = -jnp.minimum(cx_in[1].astype(F32), 0.0)
            leaves = jnp.maximum(columns[8], 0.0)
        else:
            from_east = jnp.maximum(cx_in[0].astype(F32), 0.0)
            from_west = -jnp.minimum(columns[2], 0.0)
            leaves = -jnp.minimum(columns[9], 0.0)
        centre = 1.0 - jnp.abs(cx) - jnp.abs(cy) - up - down
        return centre, up, down, from_east, from_west, north, south, leaves

    def flux_copy(side, part):
        cut = pl.ds(part * half, half)
        return pltpu.make_async_remote_copy(
            src_ref=flux_out.at[side, cut],
            dst_ref=halo_ref.at[side, cut],
            send_sem=fsend.at[side, part],
            recv_sem=frecv.at[side, part],
            device_id=((west, east)[side], rank),
            device_id_type=MESH,
        )

    halves = 2 if tracers % 2 == 0 else 1
    half = tracers // halves
    flux_copies = []
    for side in (0, 1):
        centre, up, down, from_east, from_west, north, south, leaves = edge_coeffs(side)
        top = lax.broadcasted_iota(jnp.int32, centre.shape, 0) == levels - 1
        c = (0, last)[side]

        def edge(t, _):
            x = edges[(0, 3)[side], t]
            if side == 0:
                e, w = edges[1, t], lam_in[1, t].astype(F32)
            else:
                e, w = lam_in[0, t].astype(F32), edges[2, t]
            out = x * centre + shifted(x, 1, 0) * up + shifted(x, -1, 0) * down
            out += e * from_east + w * from_west
            out += shifted(x, 1, 1) * north + shifted(x, -1, 1) * south
            out += jnp.where(top, rows_ref[t].astype(F32)[c : c + 1], 0.0)
            flux_out[side, t] = (out * leaves).astype(BF16)
            edges[(0, 3)[side], t] = out
            return 0

        for part in range(halves):
            lax.fori_loop(part * half, (part + 1) * half, edge, 0, unroll=True)
            copy = flux_copy(side, part)
            copy.start()
            flux_copies.append(copy)

    run_levels(levels // 2, levels, lam1, lam, met0)
    add_rows(lam1)

    def put(t, _):
        lam1[t, :, 0, :] = edges[0, t]
        lam1[t, :, last, :] = edges[3, t]
        return 0

    lax.fori_loop(0, tracers, put, 0, unroll=True)

    run_levels(0, levels, lam2, lam1, met1_ref)
    add_rows(lam2)

    for copy in gathers.values():
        copy.wait_send()
    for copy in flux_copies:
        copy.wait()


def add_halo(lam_ref, halo_ref, out_ref, halo):
    tracers, levels, lons, _ = lam_ref.shape
    held = out_ref.shape[1]
    step = pl.program_id(0)

    @pl.when(step == 0)
    def _():
        halo[...] = halo_ref[...].astype(F32)

    row = lax.broadcasted_iota(jnp.int32, lam_ref.shape[2:], 0)

    def level(n, _):
        k = step * held + n
        for t in range(tracers):
            out = lam_ref[t, k]
            out += jnp.where(row == lons - 1, halo[0, t, pl.ds(k, 1), :], 0.0)
            out += jnp.where(row == 0, halo[1, t, pl.ds(k, 1), :], 0.0)
            out_ref[t, n] = out
        return 0

    lax.fori_loop(0, held, level, 0)


def per_device(tiles, ranks, adjoint_state, met_fields, forcing, cluster_ids, hour_index):
    tracers, levels, lons, lats = adjoint_state.shape
    fields = met_fields.shape[1]
    vmem = pl.BlockSpec(memory_space=pltpu.VMEM)
    hbm = pl.BlockSpec(memory_space=pltpu.HBM)
    both = (2, tracers, levels, lats)
    arrays = (hour_index, cluster_ids, adjoint_state, met_fields, forcing)
    arrays = [pltpu.with_memory_space_constraint(x, pltpu.HBM) for x in arrays]
    lam2, halo = pl.pallas_call(
        functools.partial(both_steps, tiles, ranks),
        out_shape=(
            jax.ShapeDtypeStruct(adjoint_state.shape, F32),
            jax.ShapeDtypeStruct(both, BF16),
        ),
        in_specs=[hbm] * 5,
        out_specs=(vmem,) * 2,
        scratch_shapes=[
            pltpu.VMEM((fields, levels, lons, lats), BF16),
            pltpu.VMEM((tracers, lons, lats), BF16),
            pltpu.SMEM(hour_index.shape, jnp.int32),
            pltpu.SMEM(cluster_ids.shape, jnp.int32),
            pltpu.VMEM(adjoint_state.shape, F32),
            pltpu.VMEM(adjoint_state.shape, F32),
            pltpu.VMEM(met_fields.shape, BF16),
            pltpu.VMEM(forcing.shape, BF16),
            pltpu.VMEM((fields, levels, lons, lats), BF16),
            pltpu.VMEM((4, tracers, levels, lats), F32),
            pltpu.VMEM(both, BF16),
            pltpu.VMEM(both, BF16),
            pltpu.VMEM((2, levels, lats), BF16),
            pltpu.VMEM((2, levels, lats), BF16),
            pltpu.VMEM(both, BF16),
            pltpu.VMEM((10, levels, lats), F32),
            pltpu.SemaphoreType.DMA((8,)),
            pltpu.SemaphoreType.DMA((STEPS, ranks)),
            pltpu.SemaphoreType.DMA((STEPS, ranks)),
            pltpu.SemaphoreType.DMA((2, 2)),
            pltpu.SemaphoreType.DMA((2, 2)),
            pltpu.SemaphoreType.DMA((2, 2)),
            pltpu.SemaphoreType.DMA((2, 2)),
            pltpu.SemaphoreType.DMA((2, 4)),
            pltpu.SemaphoreType.DMA((2, 4)),
        ],
        compiler_params=pltpu.CompilerParams(
            collective_id=0, has_side_effects=True, vmem_limit_bytes=40 << 20
        ),
        name="both_steps",
    )(*arrays)

    held = 4 if levels % 4 == 0 else 1
    return pl.pallas_call(
        add_halo,
        grid=(levels // held,),
        out_shape=jax.ShapeDtypeStruct(adjoint_state.shape, F32),
        in_specs=[vmem] * 2,
        out_specs=pl.BlockSpec((tracers, held, lons, lats), lambda k: (0, k, 0, 0)),
        scratch_shapes=[pltpu.VMEM(both, F32)],
        compiler_params=pltpu.CompilerParams(vmem_limit_bytes=40 << 20),
        name="add_halo",
    )(lam2, halo)


def solution(mesh):
    placed = (
        P("rcpt", None, "tile", None),
        P(None, None, "rcpt", "tile", None),
        P(None, "tile", None),
        P("rcpt"),
        P(),
    )
    return jax.shard_map(
        functools.partial(per_device, mesh.shape["tile"], mesh.shape["rcpt"]),
        mesh=mesh,
        in_specs=placed,
        out_specs=P("rcpt", None, "tile", None),
        check_vma=False,
    )
```
